32 devices in a mesh: grp: 4 (over x, core), dev: 8 (over z, y).
Axes of the slice: x: 2, y: 2, z: 4, core: 2. Of those that a mesh axis runs over, the one named last changes fastest.
Arguments:
- voltages: bfloat16 [512, 16384], P(('grp', 'dev')), may hold values from -6 to 6
- filter_taps: float32 [4, 4096], replicated, may hold values from -0.046875 to 0.046875
- dipole_cells: int32 [512, 2], replicated, may hold values from 0 to 254
- kernel_bits: int32 [512, 2], replicated, may hold values from 1 to 3
- sky_model: float32 [2048, 256, 256], P('grp', 'dev'), may hold values from 0 to 2
Outputs:
- residual_images: float32 [2048, 256, 256], P('grp', 'dev')
- broadband: float32 [256, 256], P('dev')
The draws below stay inside these ranges and needn't reach their ends.
Inputs may be any that keep to these rules, and one draw needn't show every extreme that they name: `dipole_cells`: grid row and column of a dipole's first kernel cell; the kernel may also reach index plus one. `kernel_bits`: bit 0 gives weight 1 to the cell at the index, bit 1 to the cell at the index plus one.
All inputs are finite; a program needn't handle non-finite values.
Results may differ from the reference program's by a relative error of at most 0.005.
Values may be sent and summed in bfloat16 or wider, within the bound.
A program may use at most 192 MiB of HBM per device.

```python
import jax
import jax.numpy as jnp
from jax import lax

NFFT = 4096
CH = 2048
TAPS = 4
G = 256
FR = 1
ANTENNAS = 512
SAMPLES = 16384


def touch_ends(array, stream_key, smallest, largest):
    longest = array.shape.index(max(array.shape))
    spots = []
    for shift in (0, 1):
        where = [jax.random.randint(jax.random.fold_in(stream_key, axis), (), 0, length) for axis, length in enumerate(array.shape)]
        where[longest] = (where[longest] + shift) % array.shape[longest]
        spots.append(tuple(where))
    return array.at[spots[0]].set(smallest).at[spots[1]].set(largest)


def shard_levels(key, extent, cuts, smallest, top_value):
    factor_of = 1.0
    for dim, parts in cuts:
        steps = jax.random.uniform(jax.random.fold_in(jax.random.fold_in(key, 6), dim), (parts,), jnp.float32, smallest / len(cuts), top_value / len(cuts))
        factor_of = factor_of * jnp.repeat(jnp.exp(steps), extent[dim] // parts).reshape((-1,) + (1,) * (len(extent) - 1 - dim))
    return factor_of


def gaussian(key, dims, deviation, most, pieces=(), held_as=jnp.bfloat16):
    drawn = jax.random.normal(key, dims, jnp.float32) * deviation
    if len(pieces) > 0:
        drawn = shard_levels(key, dims, pieces, -0.22, 0.18) * drawn
    return jnp.clip(drawn, min=-most, max=most).astype(held_as)


def setup_inputs(seed: int = 0) -> dict:
    key_of = jax.random.split(jax.random.key(seed), 6)
    return {
        "voltages": gaussian(key_of[0], (ANTENNAS, SAMPLES), 1.0, 6.0, ((0, 32),)),
        "filter_taps": gaussian(key_of[1], (TAPS, NFFT), (TAPS * NFFT) ** -0.5, 0.046875, (), jnp.float32),
        "dipole_cells": touch_ends(jax.random.randint(key_of[2], (ANTENNAS, 2), 0, G - 1), jax.random.fold_in(key_of[2], 1), 0, (G - 1) - 1).astype(jnp.int32),
        "kernel_bits": touch_ends(jax.random.randint(key_of[3], (ANTENNAS, 2), 1, 4), jax.random.fold_in(key_of[3], 1), 1, 3).astype(jnp.int32),
        "sky_model": jnp.clip(2.0 * jax.random.uniform(key_of[4], (CH, G, G), jnp.float32) ** shard_levels(key_of[4], (CH, G, G), ((0, 4), (1, 8)), -0.2, 0.2), 0.0, 2.0),
    }


def reference(voltages, filter_taps, dipole_cells, kernel_bits, sky_model):
    segments = voltages.astype(jnp.float32).reshape(ANTENNAS, FR + TAPS - 1, NFFT)
    framed = jnp.zeros((ANTENNAS, FR, NFFT), jnp.float32)
    for tap_index in range(TAPS):
        framed = framed + filter_taps[tap_index][None, None, :] * segments[:, tap_index:tap_index + FR, :]
    spectrum = jnp.fft.fft(framed, axis=2)[:, :, :CH]
    real_part = lax.optimization_barrier(jnp.real(spectrum).astype(jnp.bfloat16)).astype(jnp.float32)
    imag_part = lax.optimization_barrier(jnp.imag(spectrum).astype(jnp.bfloat16)).astype(jnp.float32)
    low_row = (kernel_bits[:, 0] % 2).astype(jnp.float32)
    high_row = (kernel_bits[:, 0] // 2).astype(jnp.float32)
    low_col = (kernel_bits[:, 1] % 2).astype(jnp.float32)
    high_col = (kernel_bits[:, 1] // 2).astype(jnp.float32)
    block_len = min(CH, 16)
    blocks = CH // block_len
    real_blocks = real_part.reshape(ANTENNAS, FR, blocks, block_len).transpose(2, 1, 3, 0)
    imag_blocks = imag_part.reshape(ANTENNAS, FR, blocks, block_len).transpose(2, 1, 3, 0)
    sky_blocks = sky_model.reshape(blocks, block_len, G, G)

    def image_block(inputs):
        real_block, imag_block, sky_block = inputs
        grid_real = jnp.zeros((FR, block_len, G, G), jnp.float32)
        grid_imag = jnp.zeros((FR, block_len, G, G), jnp.float32)
        for shift_u, row_w in ((0, low_row), (1, high_row)):
            for shift_v, col_w in ((0, low_col), (1, high_col)):
                weight = row_w * col_w
                rows_at = dipole_cells[:, 0] + shift_u
                cols_at = dipole_cells[:, 1] + shift_v
                grid_real = grid_real.at[:, :, rows_at, cols_at].add(real_block * weight)
                grid_imag = grid_imag.at[:, :, rows_at, cols_at].add(imag_block * weight)
        half_turn = jnp.fft.fft(grid_real + 1j * grid_imag, axis=2)
        half_real = lax.optimization_barrier(jnp.real(half_turn).astype(jnp.bfloat16)).astype(jnp.float32)
        half_imag = lax.optimization_barrier(jnp.imag(half_turn).astype(jnp.bfloat16)).astype(jnp.float32)
        sky_image = jnp.fft.fft(half_real + 1j * half_imag, axis=3)
        power_sum = jnp.sum(jnp.real(sky_image) ** 2 + jnp.imag(sky_image) ** 2, axis=0)
        return power_sum / (FR * ANTENNAS) - sky_block

    residual_images = lax.map(image_block, (real_blocks, imag_blocks, sky_blocks)).reshape(CH, G, G)
    broadband = jnp.mean(residual_images, axis=0)
    return residual_images, broadband
```

```python
import functools
import math

import jax
import jax.numpy as jnp
import numpy as np
from jax import lax
from jax.experimental import pallas as pl
from jax.experimental.pallas import tpu as pltpu
from jax.sharding import PartitionSpec as P


def stage_tables(points):
    first = 1 << (int(math.log2(points)) // 2)
    second = points // first
    k1 = np.arange(first)
    n2 = np.arange(second)
    k2 = np.arange(second // 2)
    inner = np.exp(-2j * np.pi * np.outer(k1, k1) / first)
    twiddle = np.exp(-2j * np.pi * np.outer(k1, n2) / points)
    outer = np.exp(-2j * np.pi * np.outer(k2, n2) / second)
    as_pair = lambda z: np.stack([z.real, z.imag]).astype(np.float32)
    return as_pair(inner), as_pair(twiddle), as_pair(outer)


def channelize(voltages, filter_taps):
    tap_count, points = filter_taps.shape
    dipoles = voltages.shape[0]
    segments = voltages.reshape(dipoles, -1, points)
    frame_count = segments.shape[1] - tap_count + 1
    framed = jnp.zeros((dipoles, frame_count, points), jnp.float32)
    for tap in range(tap_count):
        framed = framed + filter_taps[tap][None, None, :] * segments[
            :, tap : tap + frame_count, :
        ].astype(jnp.float32)
    inner, twiddle, outer = stage_tables(points)
    first, second = twiddle.shape[1:]
    grid = framed.reshape(dipoles, frame_count, first, second)
    mid = jnp.einsum("qkn,afnm->qafkm", inner, grid, precision=lax.Precision.HIGHEST)
    turned = jnp.stack(
        [
            mid[0] * twiddle[0] - mid[1] * twiddle[1],
            mid[0] * twiddle[1] + mid[1] * twiddle[0],
        ]
    )
    full = np.stack([np.stack([outer[0], -outer[1]]), np.stack([outer[1], outer[0]])])
    spectra = jnp.einsum("pqjm,qafkm->pfajk", full, turned, precision=lax.Precision.HIGHEST)
    return spectra.astype(jnp.bfloat16).reshape(2, frame_count, dipoles, points // 2)


def phase(product, length):
    angle = (product % length).astype(jnp.float32) * (2.0 * math.pi / length)
    return jnp.cos(angle), jnp.sin(angle)


def row_factors(cells, bits, first_row, rows, length, scale):
    out = first_row + lax.broadcasted_iota(jnp.int32, (rows, cells.shape[0]), 0)
    low = (bits % 2).astype(jnp.float32) * scale
    high = (bits // 2).astype(jnp.float32) * scale
    cos_low, sin_low = phase(out * cells[None, :], length)
    cos_high, sin_high = phase(out * (cells[None, :] + 1), length)
    return jnp.stack([low * cos_low + high * cos_high, -(low * sin_low + high * sin_high)])


def col_factors(cells, bits, length):
    half = length // 2
    low = (bits % 2).astype(jnp.float32)[:, None]
    high = (bits // 2).astype(jnp.float32)[:, None]
    lane = lax.broadcasted_iota(jnp.int32, (cells.shape[0], half), 1)
    cos_low, sin_low = phase(lane * cells[:, None], length)
    cos_high, sin_high = phase((lane * (cells[:, None] + 1)), length)
    real = low * cos_low + high * cos_high
    imag = -(low * sin_low + high * sin_high)
    parity = (1 - 2 * (cells % 2)).astype(jnp.float32)[:, None]
    middle = low * parity - high * parity
    imag = jnp.where(lane == 0, middle, imag)
    return jnp.concatenate([real, imag], axis=1).astype(jnp.bfloat16)


def image_kernel(chunk, s_ref, r_ref, t_ref, sky_ref, out_ref, sum_ref, x_ref):
    step = pl.program_id(0)
    block, rows, length = sky_ref.shape
    half = length // 2
    group = chunk * rows

    @pl.when(step == 0)
    def _():
        sum_ref[...] = jnp.zeros_like(sum_ref)

    lane = lax.broadcasted_iota(jnp.int32, (group, half), 1)
    mirror = (half - lane) % half
    ends = lane == 0
    table = t_ref[...]
    total_low = jnp.zeros((rows, half), jnp.float32)
    total_high = jnp.zeros((rows, half), jnp.float32)
    for c in range(block // chunk):
        slot = c % 2
        row_re = r_ref[0]
        row_im = r_ref[1]
        for i in range(chunk):
            k = c * chunk + i
            s_re = s_ref[0, k : k + 1, :]
            s_im = s_ref[1, k : k + 1, :]
            x_ref[slot, i * rows : (i + 1) * rows, :] = (s_re * row_re - s_im * row_im).astype(
                jnp.bfloat16
            )
            x_ref[slot, group + i * rows : group + (i + 1) * rows, :] = (
                s_re * row_im + s_im * row_re
            ).astype(jnp.bfloat16)
        y = jnp.dot(x_ref[slot], table, preferred_element_type=jnp.float32)
        re_cos, re_sin = y[:group, :half], y[:group, half:]
        im_cos, im_sin = y[group:, :half], y[group:, half:]
        own = re_cos * re_cos + im_cos * im_cos
        other = re_sin * re_sin + im_sin * im_sin
        cross = 2.0 * (re_cos * im_sin - im_cos * re_sin)
        both = own + other
        low = jnp.where(ends, own, both - cross)
        high = jnp.where(ends, other, both + cross)
        high = jnp.take_along_axis(high, mirror, axis=1, mode="promise_in_bounds")
        ks = slice(c * chunk, (c + 1) * chunk)
        low = low.reshape(chunk, rows, half) - sky_ref[ks, :, :half]
        high = high.reshape(chunk, rows, half) - sky_ref[ks, :, half:]
        out_ref[ks, :, :half] = low
        out_ref[ks, :, half:] = high
        total_low = total_low + jnp.sum(low, axis=0)
        total_high = total_high + jnp.sum(high, axis=0)
    sum_ref[:, :half] += total_low
    sum_ref[:, half:] += total_high


def image(spectra, row_table, col_table, sky_model):
    channels, rows, length = sky_model.shape
    dipoles = spectra.shape[2]
    block = min(channels, 32)
    chunk = min(block, 8)
    macs = channels * rows * 2 * dipoles * length
    return pl.pallas_call(
        functools.partial(image_kernel, chunk),
        grid=(channels // block,),
        in_specs=[
            pl.BlockSpec((2, block, dipoles), lambda i: (0, i, 0)),
            pl.BlockSpec((2, rows, dipoles), lambda i: (0, 0, 0)),
            pl.BlockSpec((dipoles, length), lambda i: (0, 0)),
            pl.BlockSpec((block, rows, length), lambda i: (i, 0, 0)),
        ],
        out_specs=[
            pl.BlockSpec((block, rows, length), lambda i: (i, 0, 0)),
            pl.BlockSpec((rows, length), lambda i: (0, 0)),
        ],
        out_shape=[
            jax.ShapeDtypeStruct(sky_model.shape, jnp.float32),
            jax.ShapeDtypeStruct((rows, length), jnp.float32),
        ],
        scratch_shapes=[pltpu.VMEM((2, 2 * chunk * rows, dipoles), jnp.bfloat16)],
        compiler_params=pltpu.CompilerParams(vmem_limit_bytes=40 * 2**20),
        cost_estimate=pl.CostEstimate(
            flops=2 * macs, bytes_accessed=8 * sky_model.size, transcendentals=0
        ),
    )(spectra, row_table, col_table, sky_model)


def group_major(values, groups, members):
    return values.reshape(groups, members, -1, 2).transpose(1, 0, 2, 3).reshape(values.shape)


def body(voltages, filter_taps, dipole_cells, kernel_bits, sky_model):
    groups = lax.axis_size("grp")
    members = lax.axis_size("dev")
    dipoles = dipole_cells.shape[0]
    mine = voltages.shape[0]
    channels, rows, length = sky_model.shape
    spectra = channelize(voltages, filter_taps)
    frame_count = spectra.shape[1]
    assert frame_count == 1
    blocks = spectra.reshape(2, mine, groups, channels).transpose(2, 0, 1, 3)
    turned = lax.all_to_all(blocks, "grp", split_axis=0, concat_axis=0, tiled=True)
    everyone = lax.all_gather(turned, "dev", axis=0, tiled=True)
    everyone = everyone.transpose(1, 3, 0, 2).reshape(2, channels, dipoles).astype(jnp.float32)
    cells = group_major(dipole_cells, groups, members)
    bits = group_major(kernel_bits, groups, members)
    scale = math.sqrt(1.0 / (frame_count * dipoles))
    first_row = lax.axis_index("dev") * rows
    row_table = row_factors(cells[:, 0], bits[:, 0], first_row, rows, length, scale)
    col_table = col_factors(cells[:, 1], bits[:, 1], length)
    residual, partial = image(everyone, row_table, col_table, sky_model)
    broadband = lax.psum(partial, "grp") / (channels * groups)
    return residual, broadband


def solution(mesh):
    in_specs = (P(("grp", "dev"), None), P(), P(), P(), P("grp", "dev", None))
    out_specs = (P("grp", "dev", None), P("dev", None))
    return jax.shard_map(body, mesh=mesh, in_specs=in_specs, out_specs=out_specs, check_vma=False)
```

```python
import functools
import math

import jax
import jax.numpy as jnp
import numpy as np
from jax import lax
from jax.experimental import pallas as pl
from jax.experimental.pallas import tpu as pltpu
from jax.sharding import PartitionSpec as P


def stage_tables(points):
    first = 1 << (int(math.log2(points)) // 2)
    second = points // first
    k1 = np.arange(first)
    n2 = np.arange(second)
    k2 = np.arange(second // 2)
    inner = np.exp(-2j * np.pi * np.outer(k1, k1) / first)
    twiddle = np.exp(-2j * np.pi * np.outer(k1, n2) / points)
    outer = np.exp(-2j * np.pi * np.outer(k2, n2) / second)
    as_pair = lambda z: np.stack([z.real, z.imag]).astype(np.float32)
    return as_pair(inner), as_pair(twiddle), as_pair(outer)


def channelize(voltages, filter_taps):
    tap_count, points = filter_taps.shape
    dipoles = voltages.shape[0]
    segments = voltages.reshape(dipoles, -1, points)
    frame_count = segments.shape[1] - tap_count + 1
    framed = jnp.zeros((dipoles, frame_count, points), jnp.float32)
    for tap in range(tap_count):
        framed = framed + filter_taps[tap][None, None, :] * segments[
            :, tap : tap + frame_count, :
        ].astype(jnp.float32)
    inner, twiddle, outer = stage_tables(points)
    first, second = twiddle.shape[1:]
    grid = framed.reshape(dipoles, frame_count, first, second)
    mid = jnp.einsum("qkn,afnm->qafkm", inner, grid, precision=lax.Precision.HIGHEST)
    turned = jnp.stack(
        [
            mid[0] * twiddle[0] - mid[1] * twiddle[1],
            mid[0] * twiddle[1] + mid[1] * twiddle[0],
        ]
    )
    full = np.stack([np.stack([outer[0], -outer[1]]), np.stack([outer[1], outer[0]])])
    spectra = jnp.einsum("pqjm,qafkm->pfajk", full, turned, precision=lax.Precision.HIGHEST)
    return spectra.astype(jnp.bfloat16).reshape(2, frame_count, dipoles, points // 2)


def phase(product, length):
    angle = (product % length).astype(jnp.float32) * (2.0 * math.pi / length)
    return jnp.cos(angle), jnp.sin(angle)


def row_factors(cells, bits, first_row, rows, length, scale):
    out = first_row + lax.broadcasted_iota(jnp.int32, (rows, cells.shape[1]), 0)
    low = (bits % 2).astype(jnp.float32) * scale
    high = (bits // 2).astype(jnp.float32) * scale
    cos_low, sin_low = phase(out * cells, length)
    cos_high, sin_high = phase(out * (cells + 1), length)
    return jnp.stack([low * cos_low + high * cos_high, -(low * sin_low + high * sin_high)])


def col_factors(cells, bits, length):
    half = length // 2
    low = (bits % 2).astype(jnp.float32)
    high = (bits // 2).astype(jnp.float32)
    lane = lax.broadcasted_iota(jnp.int32, (cells.shape[0], half), 1)
    cos_low, sin_low = phase(lane * cells, length)
    cos_high, sin_high = phase(lane * (cells + 1), length)
    real = low * cos_low + high * cos_high
    imag = -(low * sin_low + high * sin_high)
    parity = (1 - 2 * (cells % 2)).astype(jnp.float32)
    middle = low * parity - high * parity
    imag = jnp.where(lane == 0, middle, imag)
    return jnp.concatenate([real, imag], axis=1).astype(jnp.bfloat16)


def image_kernel(chunk, s_ref, r_ref, t_ref, sky_ref, out_ref, sum_ref, x_ref):
    step = pl.program_id(0)
    block, rows, length = sky_ref.shape
    half = length // 2
    group = chunk * rows

    @pl.when(step == 0)
    def _():
        sum_ref[...] = jnp.zeros_like(sum_ref)

    lane = lax.broadcasted_iota(jnp.int32, (group, half), 1)
    mirror = (half - lane) % half
    ends = lane == 0
    table = t_ref[...]
    total_low = jnp.zeros((rows, half), jnp.float32)
    total_high = jnp.zeros((rows, half), jnp.float32)
    for c in range(block // chunk):
        slot = c % 2
        row_re = r_ref[0]
        row_im = r_ref[1]
        for i in range(chunk):
            k = c * chunk + i
            s_re = s_ref[0, k : k + 1, :]
            s_im = s_ref[1, k : k + 1, :]
            x_ref[slot, i * rows : (i + 1) * rows, :] = (s_re * row_re - s_im * row_im).astype(
                jnp.bfloat16
            )
            x_ref[slot, group + i * rows : group + (i + 1) * rows, :] = (
                s_re * row_im + s_im * row_re
            ).astype(jnp.bfloat16)
        y = jnp.dot(x_ref[slot], table, preferred_element_type=jnp.float32)
        re_cos, re_sin = y[:group, :half], y[:group, half:]
        im_cos, im_sin = y[group:, :half], y[group:, half:]
        own = re_cos * re_cos + im_cos * im_cos
        other = re_sin * re_sin + im_sin * im_sin
        cross = 2.0 * (re_cos * im_sin - im_cos * re_sin)
        both = own + other
        low = jnp.where(ends, own, both - cross)
        high = jnp.where(ends, other, both + cross)
        high = jnp.take_along_axis(high, mirror, axis=1, mode="promise_in_bounds")
        ks = slice(c * chunk, (c + 1) * chunk)
        low = low.reshape(chunk, rows, half) - sky_ref[ks, :, :half]
        high = high.reshape(chunk, rows, half) - sky_ref[ks, :, half:]
        out_ref[ks, :, :half] = low
        out_ref[ks, :, half:] = high
        total_low = total_low + jnp.sum(low, axis=0)
        total_high = total_high + jnp.sum(high, axis=0)
    sum_ref[:, :half] += total_low
    sum_ref[:, half:] += total_high


def image(spectra, row_table, col_table, sky_model):
    channels, rows, length = sky_model.shape
    dipoles = spectra.shape[2]
    block = min(channels, 32)
    chunk = min(block, 8)
    macs = channels * rows * 2 * dipoles * length
    return pl.pallas_call(
        functools.partial(image_kernel, chunk),
        grid=(channels // block,),
        in_specs=[
            pl.BlockSpec((2, block, dipoles), lambda i: (0, i, 0)),
            pl.BlockSpec((2, rows, dipoles), lambda i: (0, 0, 0)),
            pl.BlockSpec((dipoles, length), lambda i: (0, 0)),
            pl.BlockSpec((block, rows, length), lambda i: (i, 0, 0)),
        ],
        out_specs=[
            pl.BlockSpec((block, rows, length), lambda i: (i, 0, 0)),
            pl.BlockSpec((rows, length), lambda i: (0, 0)),
        ],
        out_shape=[
            jax.ShapeDtypeStruct(sky_model.shape, jnp.float32),
            jax.ShapeDtypeStruct((rows, length), jnp.float32),
        ],
        scratch_shapes=[pltpu.VMEM((2, 2 * chunk * rows, dipoles), jnp.bfloat16)],
        compiler_params=pltpu.CompilerParams(vmem_limit_bytes=40 * 2**20),
        cost_estimate=pl.CostEstimate(
            flops=2 * macs, bytes_accessed=8 * sky_model.size, transcendentals=0
        ),
    )(spectra, row_table, col_table, sky_model)


MESH = pl.DeviceIdType.MESH


def barrier_with(peers):
    barrier = pltpu.get_barrier_semaphore()
    for condition, device in peers:
        if condition is None:
            pl.semaphore_signal(barrier, inc=1, device_id=device, device_id_type=MESH)
        else:

            @pl.when(condition)
            def _(device=device):
                pl.semaphore_signal(barrier, inc=1, device_id=device, device_id_type=MESH)

    count = sum(1 for condition, _ in peers if condition is None)
    for condition, _ in peers:
        if condition is not None:
            count = count + condition.astype(jnp.int32)
    pl.semaphore_wait(barrier, count)


def gather_kernel(
    groups, members, line, scale,
    blocks_ref, row_cells_ref, col_cells_ref, s_ref, r_ref, t_ref,
    held, own_send, own_recv, send_sem, recv_sem, inner_send,
):
    g = lax.axis_index("grp")
    d = lax.axis_index("dev")
    inner = members // line
    z = d // inner
    y = d % inner
    up, down = z < line - 1, z > 0

    def at(group, z_at, y_at):
        return (group, z_at * inner + y_at)

    group_peers = [lax.rem(g + i, groups) for i in range(1, groups)]
    inner_peers = [lax.rem(y + i, inner) for i in range(1, inner)]
    barrier_with(
        [(None, at(p, z, y)) for p in group_peers]
        + [(None, at(g, z, p)) for p in inner_peers]
        + [(up, at(g, z + 1, y)), (down, at(g, z - 1, y))]
    )

    own = []
    for i, p in enumerate(group_peers):
        copy = pltpu.make_async_remote_copy(
            src_ref=blocks_ref.at[p], dst_ref=held.at[d, g],
            send_sem=own_send.at[i], recv_sem=own_recv.at[i],
            device_id=at(p, z, y), device_id_type=MESH,
        )
        copy.start()
        own.append(copy)
    held[d, g] = blocks_ref[g]

    rows = r_ref.shape[1]
    length = t_ref.shape[1]
    r_ref[...] = row_factors(
        row_cells_ref[0:1, :], row_cells_ref[1:2, :], d * rows, rows, length, scale
    )
    for copy in own:
        copy.wait_recv()

    def line_copy(step, slot):
        side = 0 if step > 0 else 1
        return pltpu.make_async_remote_copy(
            src_ref=held.at[slot], dst_ref=held.at[slot],
            send_sem=send_sem.at[side, slot], recv_sem=recv_sem.at[slot],
            device_id=at(g, z + step, y), device_id_type=MESH,
        )

    def both_ways(slot):
        @pl.when(up)
        def _():
            line_copy(1, slot).start()

        @pl.when(down)
        def _():
            line_copy(-1, slot).start()

    crossing = []
    for i, p in enumerate(inner_peers):
        copy = pltpu.make_async_remote_copy(
            src_ref=held.at[d], dst_ref=held.at[d],
            send_sem=inner_send.at[i], recv_sem=recv_sem.at[d],
            device_id=at(g, z, p), device_id_type=MESH,
        )
        copy.start()
        crossing.append(copy)
    both_ways(d)

    def arrived(slot):
        pltpu.make_async_remote_copy(
            src_ref=held.at[slot], dst_ref=held.at[slot],
            send_sem=send_sem.at[0, slot], recv_sem=recv_sem.at[slot],
            device_id=at(g, z, y), device_id_type=MESH,
        ).wait_recv()

    columns = [y] + inner_peers
    for p in inner_peers:
        slot = z * inner + p
        arrived(slot)
        both_ways(slot)
    t_ref[...] = col_factors(col_cells_ref[:, 0:1], col_cells_ref[:, 1:2], length)
    for reach in range(1, line):
        for p in columns:

            @pl.when(z >= reach)
            def _(p=p):
                slot = (z - reach) * inner + p
                arrived(slot)

                @pl.when(up)
                def _():
                    line_copy(1, slot).start()

            @pl.when(z + reach < line)
            def _(p=p):
                slot = (z + reach) * inner + p
                arrived(slot)

                @pl.when(down)
                def _():
                    line_copy(-1, slot).start()

    dipoles = s_ref.shape[2]
    for q in range(2):
        part = held[:, :, q].reshape(dipoles, s_ref.shape[1])
        s_ref[q] = part.astype(jnp.float32).T

    for copy in own + crossing:
        copy.wait_send()
    for reach in range(line):
        for p in columns:

            @pl.when(up & (z >= reach))
            def _(p=p):
                line_copy(1, (z - reach) * inner + p).wait_send()

            @pl.when(down & (z + reach < line))
            def _(p=p):
                line_copy(-1, (z + reach) * inner + p).wait_send()


def gather(blocks, row_cells, col_cells, rows, length, members, scale):
    groups, _, mine, channels = blocks.shape
    dipoles = col_cells.shape[0]
    line = math.gcd(members, 4)
    inner = members // line
    dma = pltpu.SemaphoreType.DMA
    vmem = pl.BlockSpec(memory_space=pltpu.VMEM)
    return pl.pallas_call(
        functools.partial(gather_kernel, groups, members, line, scale),
        in_specs=[vmem] * 3,
        out_specs=[vmem] * 3,
        out_shape=[
            jax.ShapeDtypeStruct((2, channels, dipoles), jnp.float32),
            jax.ShapeDtypeStruct((2, rows, dipoles), jnp.float32),
            jax.ShapeDtypeStruct((dipoles, length), jnp.bfloat16),
        ],
        scratch_shapes=[
            pltpu.VMEM((members, groups, 2, mine, channels), jnp.bfloat16),
            dma((max(groups - 1, 1),)),
            dma((max(groups - 1, 1),)),
            dma((2, members)),
            dma((members,)),
            dma((max(inner - 1, 1),)),
        ],
        compiler_params=pltpu.CompilerParams(
            collective_id=0, has_side_effects=True, vmem_limit_bytes=40 * 2**20
        ),
    )(blocks, row_cells, col_cells)


def total_kernel(groups, scale, part_ref, out_ref, held, send_sem, recv_sem):
    g = lax.axis_index("grp")
    d = lax.axis_index("dev")
    peers = [lax.rem(g + i, groups) for i in range(1, groups)]
    barrier_with([(None, (p, d)) for p in peers])
    copies = []
    for i, p in enumerate(peers):
        copy = pltpu.make_async_remote_copy(
            src_ref=part_ref, dst_ref=held.at[i],
            send_sem=send_sem.at[i], recv_sem=recv_sem.at[i],
            device_id=(p, d), device_id_type=MESH,
        )
        copy.start()
        copies.append(copy)
    total = part_ref[...]
    for i, copy in enumerate(copies):
        copy.wait_recv()
        total = total + held[i]
    out_ref[...] = total * scale
    for copy in copies:
        copy.wait_send()


def group_total(part, groups, scale):
    vmem = pl.BlockSpec(memory_space=pltpu.VMEM)
    dma = pltpu.SemaphoreType.DMA
    return pl.pallas_call(
        functools.partial(total_kernel, groups, scale),
        in_specs=[vmem],
        out_specs=vmem,
        out_shape=jax.ShapeDtypeStruct(part.shape, jnp.float32),
        scratch_shapes=[
            pltpu.VMEM((groups - 1,) + part.shape, jnp.float32),
            dma((groups - 1,)),
            dma((groups - 1,)),
        ],
        compiler_params=pltpu.CompilerParams(collective_id=1, has_side_effects=True),
    )(part)


def group_major(values, groups, members):
    return values.reshape(groups, members, -1, 2).transpose(1, 0, 2, 3).reshape(values.shape)


def body(voltages, filter_taps, dipole_cells, kernel_bits, sky_model):
    groups = lax.axis_size("grp")
    members = lax.axis_size("dev")
    dipoles = dipole_cells.shape[0]
    mine = voltages.shape[0]
    channels, rows, length = sky_model.shape
    spectra = channelize(voltages, filter_taps)
    frame_count = spectra.shape[1]
    assert frame_count == 1
    blocks = spectra.reshape(2, mine, groups, channels).transpose(2, 0, 1, 3)
    cells = group_major(dipole_cells, groups, members)
    bits = group_major(kernel_bits, groups, members)
    row_cells = jnp.stack([cells[:, 0], bits[:, 0]])
    col_cells = jnp.stack([cells[:, 1], bits[:, 1]], axis=1)
    scale = math.sqrt(1.0 / (frame_count * dipoles))
    everyone, row_table, col_table = gather(
        blocks, row_cells, col_cells, rows, length, members, scale
    )
    residual, partial = image(everyone, row_table, col_table, sky_model)
    broadband = group_total(partial, groups, 1.0 / (channels * groups))
    return residual, broadband


def solution(mesh):
    in_specs = (P(("grp", "dev"), None), P(), P(), P(), P("grp", "dev", None))
    out_specs = (P("grp", "dev", None), P("dev", None))
    return jax.shard_map(body, mesh=mesh, in_specs=in_specs, out_specs=out_specs, check_vma=False)
```

```python
import functools
import math

import jax
import jax.numpy as jnp
import numpy as np
from jax import lax
from jax.experimental import pallas as pl
from jax.experimental.pallas import tpu as pltpu
from jax.sharding import PartitionSpec as P


def stage_tables(points):
    first = 1 << (int(math.log2(points)) // 2)
    second = points // first
    k1 = np.arange(first)
    n2 = np.arange(second)
    k2 = np.arange(second // 2)
    inner = np.exp(-2j * np.pi * np.outer(k1, k1) / first)
    twiddle = np.exp(-2j * np.pi * np.outer(k1, n2) / points)
    outer = np.exp(-2j * np.pi * np.outer(k2, n2) / second)
    as_pair = lambda z: np.stack([z.real, z.imag]).astype(np.float32)
    return as_pair(inner), as_pair(twiddle), as_pair(outer)


def channelize(voltages, filter_taps):
    tap_count, points = filter_taps.shape
    dipoles = voltages.shape[0]
    segments = voltages.reshape(dipoles, -1, points)
    frame_count = segments.shape[1] - tap_count + 1
    framed = jnp.zeros((dipoles, frame_count, points), jnp.float32)
    for tap in range(tap_count):
        framed = framed + filter_taps[tap][None, None, :] * segments[
            :, tap : tap + frame_count, :
        ].astype(jnp.float32)
    inner, twiddle, outer = stage_tables(points)
    first, second = twiddle.shape[1:]
    grid = framed.reshape(dipoles, frame_count, first, second)
    mid = jnp.einsum("qkn,afnm->qafkm", inner, grid, precision=lax.Precision.HIGHEST)
    turned = jnp.stack(
        [
            mid[0] * twiddle[0] - mid[1] * twiddle[1],
            mid[0] * twiddle[1] + mid[1] * twiddle[0],
        ]
    )
    full = np.stack([np.stack([outer[0], -outer[1]]), np.stack([outer[1], outer[0]])])
    spectra = jnp.einsum("pqjm,qafkm->pfajk", full, turned, precision=lax.Precision.HIGHEST)
    return spectra.astype(jnp.bfloat16).reshape(2, frame_count, dipoles, points // 2)


def grid_tables(length):
    half = length // 2
    index = np.arange(length)
    angle = (np.outer(index, index) % length) * (2.0 * np.pi / length)
    rows = np.stack([np.cos(angle), -np.sin(angle)])
    cols = np.concatenate(
        [rows[0][:, :half], rows[0][:, half : half + 1], rows[1][:, 1:half]], axis=1
    )
    return rows.astype(np.float32), cols.astype(np.float32)


def one_hot(cells, bits, axis, length):
    shape = (length, cells.shape[1]) if axis == 0 else (cells.shape[0], length)
    index = lax.broadcasted_iota(jnp.int32, shape, axis)
    low = (bits % 2).astype(jnp.float32)
    high = (bits // 2).astype(jnp.float32)
    weight = jnp.where(index == cells, low, 0.0) + jnp.where(index == cells + 1, high, 0.0)
    return weight.astype(jnp.bfloat16)


def split(table):
    upper = table.astype(jnp.bfloat16)
    return upper, (table - upper.astype(jnp.float32)).astype(jnp.bfloat16)


def dot(lhs, rhs):
    return jnp.dot(lhs, rhs, preferred_element_type=jnp.float32)


def image_kernel(chunk, s_ref, r_ref, t_ref, sky_ref, out_ref, sum_ref, x_ref):
    step = pl.program_id(0)
    block, rows, length = sky_ref.shape
    half = length // 2
    group = chunk * rows

    @pl.when(step == 0)
    def _():
        sum_ref[...] = jnp.zeros_like(sum_ref)

    lane = lax.broadcasted_iota(jnp.int32, (group, half), 1)
    mirror = (half - lane) % half
    ends = lane == 0
    table = t_ref[...]
    total_low = jnp.zeros((rows, half), jnp.float32)
    total_high = jnp.zeros((rows, half), jnp.float32)
    for c in range(block // chunk):
        slot = c % 2
        row_re = r_ref[0]
        row_im = r_ref[1]
        for i in range(chunk):
            k = c * chunk + i
            s_re = s_ref[0, k : k + 1, :]
            s_im = s_ref[1, k : k + 1, :]
            x_ref[slot, i * rows : (i + 1) * rows, :] = (s_re * row_re - s_im * row_im).astype(
                jnp.bfloat16
            )
            x_ref[slot, group + i * rows : group + (i + 1) * rows, :] = (
                s_re * row_im + s_im * row_re
            ).astype(jnp.bfloat16)
        y = jnp.dot(x_ref[slot], table, preferred_element_type=jnp.float32)
        re_cos, re_sin = y[:group, :half], y[:group, half:]
        im_cos, im_sin = y[group:, :half], y[group:, half:]
        own = re_cos * re_cos + im_cos * im_cos
        other = re_sin * re_sin + im_sin * im_sin
        cross = 2.0 * (re_cos * im_sin - im_cos * re_sin)
        both = own + other
        low = jnp.where(ends, own, both - cross)
        high = jnp.where(ends, other, both + cross)
        high = jnp.take_along_axis(high, mirror, axis=1, mode="promise_in_bounds")
        ks = slice(c * chunk, (c + 1) * chunk)
        low = low.reshape(chunk, rows, half) - sky_ref[ks, :, :half]
        high = high.reshape(chunk, rows, half) - sky_ref[ks, :, half:]
        out_ref[ks, :, :half] = low
        out_ref[ks, :, half:] = high
        total_low = total_low + jnp.sum(low, axis=0)
        total_high = total_high + jnp.sum(high, axis=0)
    sum_ref[:, :half] += total_low
    sum_ref[:, half:] += total_high


def image(spectra, row_table, col_table, sky_model):
    channels, rows, length = sky_model.shape
    dipoles = spectra.shape[2]
    block = min(channels, 64)
    chunk = min(block, 8)
    macs = channels * rows * 2 * dipoles * length
    return pl.pallas_call(
        functools.partial(image_kernel, chunk),
        grid=(channels // block,),
        in_specs=[
            pl.BlockSpec((2, block, dipoles), lambda i: (0, i, 0)),
            pl.BlockSpec((2, rows, dipoles), lambda i: (0, 0, 0)),
            pl.BlockSpec((dipoles, length), lambda i: (0, 0)),
            pl.BlockSpec((block, rows, length), lambda i: (i, 0, 0)),
        ],
        out_specs=[
            pl.BlockSpec((block, rows, length), lambda i: (i, 0, 0)),
            pl.BlockSpec((rows, length), lambda i: (0, 0)),
        ],
        out_shape=[
            jax.ShapeDtypeStruct(sky_model.shape, jnp.float32),
            jax.ShapeDtypeStruct((rows, length), jnp.float32),
        ],
        scratch_shapes=[pltpu.VMEM((2, 2 * chunk * rows, dipoles), jnp.bfloat16)],
        compiler_params=pltpu.CompilerParams(vmem_limit_bytes=40 * 2**20),
        cost_estimate=pl.CostEstimate(
            flops=2 * macs, bytes_accessed=8 * sky_model.size, transcendentals=0
        ),
    )(spectra, row_table, col_table, sky_model)


MESH = pl.DeviceIdType.MESH


def barrier_with(peers):
    barrier = pltpu.get_barrier_semaphore()
    for condition, device in peers:
        if condition is None:
            pl.semaphore_signal(barrier, inc=1, device_id=device, device_id_type=MESH)
        else:

            @pl.when(condition)
            def _(device=device):
                pl.semaphore_signal(barrier, inc=1, device_id=device, device_id_type=MESH)

    count = sum(1 for condition, _ in peers if condition is None)
    for condition, _ in peers:
        if condition is not None:
            count = count + condition.astype(jnp.int32)
    pl.semaphore_wait(barrier, count)


def gather_kernel(
    groups, members, line, scale,
    blocks_ref, row_cells_ref, col_cells_ref, row_dft_ref, col_dft_ref,
    s_ref, r_ref, t_ref,
    held, own_send, own_recv, line_send, cross_send, recv_sem,
):
    g = lax.axis_index("grp")
    d = lax.axis_index("dev")
    inner = members // line
    z = d // inner
    y = d % inner
    up, down = z < line - 1, z > 0

    def at(group, z_at, y_at):
        return (group, z_at * inner + y_at)

    group_peers = [lax.rem(g + i, groups) for i in range(1, groups)]
    inner_peers = [lax.rem(y + i, inner) for i in range(1, inner)]
    barrier_with(
        [(None, at(p, z, y)) for p in group_peers]
        + [(None, at(g, z, p)) for p in inner_peers]
        + [(up, at(g, z + 1, y)), (down, at(g, z - 1, y))]
    )

    own = []
    for i, p in enumerate(group_peers):
        copy = pltpu.make_async_remote_copy(
            src_ref=blocks_ref.at[p], dst_ref=held.at[:, d, g],
            send_sem=own_send.at[i], recv_sem=own_recv.at[i],
            device_id=at(p, z, y), device_id_type=MESH,
        )
        copy.start()
        own.append(copy)
    held[:, d, g] = blocks_ref[g]

    rows = r_ref.shape[1]
    length = t_ref.shape[1]
    hot = one_hot(row_cells_ref[0:1, :], row_cells_ref[1:2, :], 0, length)
    for q in range(2):
        upper, lower = split(row_dft_ref[q, pl.ds(pl.multiple_of(d * rows, rows), rows), :])
        r_ref[q] = (dot(upper, hot) + dot(lower, hot)) * scale
    for copy in own:
        copy.wait_recv()

    def line_copy(step, q, slot):
        side = 0 if step > 0 else 1
        return pltpu.make_async_remote_copy(
            src_ref=held.at[q, slot], dst_ref=held.at[q, slot],
            send_sem=line_send.at[side, q, slot], recv_sem=recv_sem.at[q, slot],
            device_id=at(g, z + step, y), device_id_type=MESH,
        )

    def along(step, q, slot):
        @pl.when(up if step > 0 else down)
        def _():
            line_copy(step, q, slot).start()

    def cross_copy(i, q, slot):
        return pltpu.make_async_remote_copy(
            src_ref=held.at[q, slot], dst_ref=held.at[q, slot],
            send_sem=cross_send.at[i, q, slot], recv_sem=recv_sem.at[q, slot],
            device_id=at(g, z, inner_peers[i]), device_id_type=MESH,
        )

    def across(q, slot):
        for i in range(inner - 1):
            cross_copy(i, q, slot).start()

    def arrived(q, slot):
        line_copy(1, q, slot).wait_recv()

    across(0, d)
    along(1, 1, d)
    along(-1, 1, d)
    along(1, 0, d)
    along(-1, 0, d)
    across(1, d)
    for p in inner_peers:
        slot = z * inner + p
        arrived(0, slot)
        along(1, 0, slot)
        along(-1, 0, slot)
    upper, lower = split(col_dft_ref[...])
    hot = one_hot(col_cells_ref[:, 0:1], col_cells_ref[:, 1:2], 1, length)
    t_ref[...] = (dot(hot, upper) + dot(hot, lower)).astype(jnp.bfloat16)
    for reach in range(1, line):
        for q, p in [(1, y), (0, y)] + [(0, p) for p in inner_peers]:

            @pl.when(z >= reach)
            def _(q=q, p=p):
                slot = (z - reach) * inner + p
                arrived(q, slot)
                along(1, q, slot)
                if q == 1:
                    across(q, slot)

            @pl.when(z + reach < line)
            def _(q=q, p=p):
                slot = (z + reach) * inner + p
                arrived(q, slot)
                along(-1, q, slot)
                if q == 1:
                    across(q, slot)

    dipoles = s_ref.shape[2]

    def turn(q):
        part = held[q].reshape(dipoles, s_ref.shape[1])
        s_ref[q] = part.astype(jnp.float32).T

    turn(0)
    for z_at in range(line):
        for p in inner_peers:
            arrived(1, z_at * inner + p)
    turn(1)

    for copy in own:
        copy.wait_send()
    for i in range(inner - 1):
        cross_copy(i, 0, d).wait_send()
        for z_at in range(line):
            cross_copy(i, 1, z_at * inner + y).wait_send()
    for reach in range(line):
        for q, p in [(1, y), (0, y)] + [(0, p) for p in inner_peers]:

            @pl.when(up & (z >= reach))
            def _(q=q, p=p):
                line_copy(1, q, (z - reach) * inner + p).wait_send()

            @pl.when(down & (z + reach < line))
            def _(q=q, p=p):
                line_copy(-1, q, (z + reach) * inner + p).wait_send()


def gather(blocks, row_cells, col_cells, rows, length, members, scale):
    groups, _, mine, channels = blocks.shape
    dipoles = col_cells.shape[0]
    line = math.gcd(members, 4)
    inner = members // line
    dma = pltpu.SemaphoreType.DMA
    vmem = pl.BlockSpec(memory_space=pltpu.VMEM)
    row_dft, col_dft = grid_tables(length)
    return pl.pallas_call(
        functools.partial(gather_kernel, groups, members, line, scale),
        in_specs=[vmem] * 5,
        out_specs=[vmem] * 3,
        out_shape=[
            jax.ShapeDtypeStruct((2, channels, dipoles), jnp.float32),
            jax.ShapeDtypeStruct((2, rows, dipoles), jnp.float32),
            jax.ShapeDtypeStruct((dipoles, length), jnp.bfloat16),
        ],
        scratch_shapes=[
            pltpu.VMEM((2, members, groups, mine, channels), jnp.bfloat16),
            dma((groups - 1,)),
            dma((groups - 1,)),
            dma((2, 2, members)),
            dma((inner - 1, 2, members)),
            dma((2, members)),
        ],
        compiler_params=pltpu.CompilerParams(
            collective_id=0, has_side_effects=True, vmem_limit_bytes=40 * 2**20
        ),
    )(blocks, row_cells, col_cells, row_dft, col_dft)


def total_kernel(groups, scale, part_ref, out_ref, held, send_sem, recv_sem):
    g = lax.axis_index("grp")
    d = lax.axis_index("dev")
    peers = [lax.rem(g + i, groups) for i in range(1, groups)]
    barrier_with([(None, (p, d)) for p in peers])
    copies = []
    for i, p in enumerate(peers):
        copy = pltpu.make_async_remote_copy(
            src_ref=part_ref, dst_ref=held.at[i],
            send_sem=send_sem.at[i], recv_sem=recv_sem.at[i],
            device_id=(p, d), device_id_type=MESH,
        )
        copy.start()
        copies.append(copy)
    total = part_ref[...]
    for i, copy in enumerate(copies):
        copy.wait_recv()
        total = total + held[i]
    out_ref[...] = total * scale
    for copy in copies:
        copy.wait_send()


def group_total(part, groups, scale):
    vmem = pl.BlockSpec(memory_space=pltpu.VMEM)
    dma = pltpu.SemaphoreType.DMA
    return pl.pallas_call(
        functools.partial(total_kernel, groups, scale),
        in_specs=[vmem],
        out_specs=vmem,
        out_shape=jax.ShapeDtypeStruct(part.shape, jnp.float32),
        scratch_shapes=[
            pltpu.VMEM((groups - 1,) + part.shape, jnp.float32),
            dma((groups - 1,)),
            dma((groups - 1,)),
        ],
        compiler_params=pltpu.CompilerParams(collective_id=1, has_side_effects=True),
    )(part)


def group_major(values, groups, members):
    return values.reshape(groups, members, -1, 2).transpose(1, 0, 2, 3).reshape(values.shape)


def body(voltages, filter_taps, dipole_cells, kernel_bits, sky_model):
    groups = lax.axis_size("grp")
    members = lax.axis_size("dev")
    dipoles = dipole_cells.shape[0]
    mine = voltages.shape[0]
    channels, rows, length = sky_model.shape
    spectra = channelize(voltages, filter_taps)
    frame_count = spectra.shape[1]
    assert frame_count == 1
    blocks = spectra.reshape(2, mine, groups, channels).transpose(2, 0, 1, 3)
    cells = group_major(dipole_cells, groups, members)
    bits = group_major(kernel_bits, groups, members)
    row_cells = jnp.stack([cells[:, 0], bits[:, 0]])
    col_cells = jnp.stack([cells[:, 1], bits[:, 1]], axis=1)
    scale = math.sqrt(1.0 / (frame_count * dipoles))
    everyone, row_table, col_table = gather(
        blocks, row_cells, col_cells, rows, length, members, scale
    )
    residual, partial = image(everyone, row_table, col_table, sky_model)
    broadband = group_total(partial, groups, 1.0 / (channels * groups))
    return residual, broadband


def solution(mesh):
    in_specs = (P(("grp", "dev"), None), P(), P(), P(), P("grp", "dev", None))
    out_specs = (P("grp", "dev", None), P("dev", None))
    return jax.shard_map(body, mesh=mesh, in_specs=in_specs, out_specs=out_specs, check_vma=False)
```
